128 devices in a mesh: side: 2 (over core), dp: 16 (over x, y), tp: 4 (over z).
Axes of the slice: x: 4, y: 4, z: 4, core: 2. Of those that a mesh axis runs over, the one named last changes fastest.
Arguments:
- hidden_in: bfloat16 [4, 1024, 4096], P(None, ('side', 'dp', 'tp')), may hold values from -6 to 6
- queries: bfloat16 [4, 1024, 4096], P(None, ('side', 'dp'), 'tp'), may hold values from -90 to 90
- new_kv: bfloat16 [4, 2, 1024, 512], P(None, None, ('side', 'dp'), 'tp'), may hold values from -5 to 5
- cache: bfloat16 [2, 1024, 128, 512], P(None, ('side', 'dp'), None, 'tp'), may hold values from -5 to 5, as said below
- lengths: int32 [1024], P(('side', 'dp')), may hold values from 2 to 124, as said below
- out_weight: bfloat16 [4096, 4096], P('tp'), may hold values from -0.375 to 0.375
- norm_gain: bfloat16 [4096], replicated, may hold values from 0.5 to 1.5
- routes: int32 [4, 1024, 8], P(None, ('side', 'dp', 'tp')), may hold values from 0 to 63, all different within a row; in each aligned block of 8 rows (0 to 7, 8 to 15, ..., all dimensions but the last counted through in order) at most 2 rows name the same one
- route_weights: float32 [4, 1024, 8], P(None, ('side', 'dp', 'tp')), may hold values from 0.1 to 1
- w_gate: bfloat16 [64, 4096, 1280], P(('dp', 'tp'), None, 'side'), may hold values from -0.09375 to 0.09375
- w_up: bfloat16 [64, 4096, 1280], P(('dp', 'tp'), None, 'side'), may hold values from -0.09375 to 0.09375
- w_down: bfloat16 [64, 1280, 4096], P(('dp', 'tp'), 'side'), may hold values from -0.15625 to 0.15625
Outputs:
- layer_out: bfloat16 [4, 1024, 4096], P(None, ('side', 'dp', 'tp'))
The draws below stay inside these ranges and needn't reach their ends.
Inputs may be any that keep to these rules, and one draw needn't show every extreme that they name: `routes`: each row names 8 different experts. Among the 8 rows of one device in one step (aligned blocks of rows, steps then requests in order) no expert is named more than 2 times, and that bound is reached. `lengths`: the largest length is reached by some request. Entries at cache positions at or past a request's length are not used.
All inputs are finite; a program needn't handle non-finite values.
Results may differ from the reference program's by a relative error of at most 0.022.
Values may be sent and summed in bfloat16 or wider, within the bound.
No kernel may reach another device: no remote copies, remote signals or barrier semaphores. Data moves between devices by JAX's collectives and lax.ppermute only.
A program may use at most 128 MiB of HBM per device.

```python
import math
import jax
import jax.numpy as jnp
import numpy as np
from jax import lax

D = 4096
H = 32
KVH = 4
HD = 128
HID = 1280
TOPK = 8
STEPS = 4
CTX = 128
TOK_DEV = 8
REQUESTS = 1024
EXPERTS = 64
HID_HALF = 640
SLOT = 2
N_SIDE = 2
N_DP = 16


def draw_cache(key, part):
    key = jax.random.fold_in(key, 11)
    first_key = jax.random.fold_in(key, 0)
    shape = (2, REQUESTS, CTX, KVH * HD)
    values = jax.random.truncated_normal(first_key, -5.0, 5.0, shape, jnp.float32)
    return values.astype(jnp.bfloat16)


def draw_queries(key, part):
    key = jax.random.fold_in(key, 12)
    first_key = jax.random.fold_in(key, 0)
    shape = (STEPS, REQUESTS, H * HD)
    values = jax.random.truncated_normal(first_key, -5.0, 5.0, shape, jnp.float32)
    return values.astype(jnp.bfloat16)


def draw_lengths(key, part):
    key = jax.random.fold_in(key, 13)
    first_key, second_key = jax.random.split(key)
    values = jax.random.randint(first_key, (REQUESTS,), 2, CTX - STEPS + 1)
    chosen = jax.random.randint(second_key, (), 0, REQUESTS)
    return values.at[chosen].set(CTX - STEPS)


def steps_of(rng, dims, cuts, least, high):
    loudness, own = 1.0, jax.random.fold_in(rng, 6)
    for dim, blocks in cuts:
        steps = jnp.exp(jax.random.uniform(jax.random.fold_in(own, dim), (blocks,), jnp.float32, least / len(cuts), high / len(cuts)))
        loudness = loudness * jnp.repeat(steps, dims[dim] // blocks).reshape([-1 if axis == dim else 1 for axis in range(len(dims))])
    return loudness


def deal_out(key, own, number, rows, amount, top, most, skew):
    order = jax.random.permutation(key, amount)
    packed, ordinary = load_shares(amount, rows * top, most, skew, True), load_shares(amount, rows * top, most, skew, False)
    places = jnp.arange(amount)

    def named(tallies, turn):
        used = int((tallies > 0).sum())
        fixed = max(1, used // 4)
        shifted = fixed + (places - fixed + turn * (used - fixed)) % max(1, amount - fixed)
        return jnp.zeros((amount,), jnp.int32).at[order[jnp.where(places < fixed, places, shifted)]].set(jnp.asarray(tallies, jnp.int32))

    tallies = jnp.where(number % 4 == 0, named(packed, number // 4), named(ordinary, number - number // 4 - 1))
    mixed = jax.random.permutation(jax.random.fold_in(own, 3), amount)
    giver, receiver = mixed[0:amount // 2 * 2:2], mixed[1:amount // 2 * 2:2]
    slack = jnp.minimum(tallies[giver] - 1, most - tallies[receiver]) // 2
    slack = jnp.where((giver == order[0]) | (receiver == order[0]) | (tallies[receiver] == 0), 0, jnp.maximum(slack, 0))
    shifted = jax.random.randint(jax.random.fold_in(own, 4), (amount // 2,), 0, 1 << 20) % (slack + 1)
    tallies = tallies.at[giver].add(-shifted).at[receiver].add(shifted)
    members = jnp.searchsorted(jnp.cumsum(tallies), jnp.arange(rows * top), side="right").astype(jnp.int32)
    table = members.reshape(top, rows).T
    table = table[jax.random.permutation(jax.random.fold_in(own, 1), rows)]
    turn = jax.random.randint(jax.random.fold_in(own, 2), (rows, 1), 0, top)
    return jnp.take_along_axis(table, (jnp.arange(top)[None, :] + turn) % top, axis=1)


def load_shares(number_of, total, most, lean, full):
    portions = [(1 << 20) // math.isqrt(standing ** lean) + 1 for standing in range(1, number_of + 1)]
    largest = most if full else min(most, max(-(-total // number_of), total * portions[0] // sum(portions)))
    least = 1 if total - largest >= number_of - 1 else 0
    given, rest = [largest] + [least] * (number_of - 1), total - largest - least * (number_of - 1)
    while rest > 0:
        movable = [i for i in range(1, number_of) if given[i] < largest] or [i for i in range(1, number_of) if given[i] < most]
        pool, left = sum([portions[i] for i in movable]), rest
        for i in movable:
            more = min(most - given[i], max(1, left * portions[i] // pool), rest)
            given[i] = given[i] + more
            rest = rest - more
    return np.array(given)


def scatter_about(key, dims, deviation, bound, cuts=(), held_as=jnp.bfloat16):
    result = deviation * jax.random.normal(key, dims, jnp.float32)
    if cuts:
        result = result * steps_of(key, dims, cuts, -0.22, 0.18)
    return jnp.clip(result, -bound, bound).astype(held_as)


def setup_inputs(seed: int = 0) -> dict:
    seeds = jax.random.split(jax.random.key(seed), 13)
    hidden_in = scatter_about(seeds[0], (STEPS, REQUESTS, D), 1.0, 6.0, ((1, 128),))
    queries = draw_queries(jax.random.fold_in(seeds[12], 71), 0)
    new_kv = scatter_about(seeds[2], (STEPS, 2, REQUESTS, KVH * HD), 1.0, 5.0, ((2, 32), (3, 4)))
    cache = draw_cache(jax.random.fold_in(seeds[12], 71), 0)
    lengths = draw_lengths(jax.random.fold_in(seeds[12], 71), 0)
    out_weight = scatter_about(seeds[5], (H * HD, D), (H * HD // 16) ** -0.5, 0.375, ((0, 4),))
    norm_gain = jnp.clip(1.0 + 0.1 * jax.random.normal(seeds[6], (D,), jnp.float32), 0.5, 1.5).astype(jnp.bfloat16)
    routes_keys = jax.random.split(jax.random.fold_in(seeds[7], 1), STEPS * REQUESTS // TOK_DEV)
    routes_turns = jax.random.permutation(jax.random.fold_in(seeds[7], 3), STEPS * REQUESTS // TOK_DEV)
    routes = jax.vmap(lambda own, number: deal_out(jax.random.fold_in(seeds[7], 2), own, number, TOK_DEV, EXPERTS, TOPK, SLOT, 2))(routes_keys, routes_turns).reshape((STEPS, REQUESTS, TOPK))
    route_weights = jnp.clip(jnp.exp(math.log(1.0) - 2.3025851 * jax.random.uniform(seeds[8], (STEPS, REQUESTS, TOPK), jnp.float32) ** steps_of(seeds[8], (STEPS, REQUESTS, TOPK), ((1, 128),), -0.2, 0.2)), 0.1, 1.0)
    w_gate = scatter_about(seeds[9], (EXPERTS, D, HID), D ** -0.5, 0.09375, ((0, 64), (2, 2)))
    w_up = scatter_about(seeds[10], (EXPERTS, D, HID), D ** -0.5, 0.09375, ((0, 64), (2, 2)))
    w_down = scatter_about(seeds[11], (EXPERTS, HID, D), HID ** -0.5, 0.15625, ((0, 64), (1, 2)))
    return {"hidden_in": hidden_in, "queries": queries, "new_kv": new_kv, "cache": cache, "lengths": lengths, "out_weight": out_weight, "norm_gain": norm_gain, "routes": routes, "route_weights": route_weights, "w_gate": w_gate, "w_up": w_up, "w_down": w_down}


EPSILON = 1e-06
NEGATIVE = -1e+30

def softmax_pair(old_scores, new_scores):
    row_max = jnp.maximum(lax.optimization_barrier(jnp.max(old_scores, axis=-1)), lax.optimization_barrier(jnp.max(new_scores, axis=-1)))
    old_exp = jnp.exp(old_scores - row_max[..., None])
    new_exp = jnp.exp(new_scores - row_max[..., None])
    row_total = lax.optimization_barrier(jnp.sum(old_exp, axis=-1)) + lax.optimization_barrier(jnp.sum(new_exp, axis=-1))
    old_probs = (old_exp / row_total[..., None]).astype(jnp.bfloat16)
    new_probs = (new_exp / row_total[..., None]).astype(jnp.bfloat16)
    return (old_probs, new_probs)

def reference(hidden_in, queries, new_kv, cache, lengths, out_weight, norm_gain, routes, route_weights, w_gate, w_up, w_down):
    group_size = H // KVH
    score_scale = 1.0 / math.sqrt(HD)
    req_block = REQUESTS // (N_SIDE * N_DP)
    block_count = REQUESTS // req_block
    keys_old = cache[0].reshape(block_count, req_block, CTX, KVH, HD)
    vals_old = cache[1].reshape(block_count, req_block, CTX, KVH, HD)
    keys_new = new_kv[:, 0].reshape(STEPS, block_count, req_block, KVH, HD).transpose(1, 0, 2, 3, 4)
    vals_new = new_kv[:, 1].reshape(STEPS, block_count, req_block, KVH, HD).transpose(1, 0, 2, 3, 4)
    lens_block = lengths.reshape(block_count, req_block)
    positions = jnp.arange(CTX, dtype=jnp.int32)
    section_iota = jnp.arange(STEPS, dtype=jnp.int32)
    source_count = REQUESTS // TOK_DEV
    assign = TOK_DEV * TOPK
    expert_iota = jnp.arange(EXPERTS, dtype=jnp.int32)
    source_index = jnp.broadcast_to(jnp.arange(source_count, dtype=jnp.int32)[:, None], (source_count, assign))
    token_index = jnp.arange(assign, dtype=jnp.int32) // TOPK
    gain = norm_gain.astype(jnp.float32)
    results = []
    for section in range(STEPS):
        query_blocks = queries[section].reshape(block_count, req_block, KVH, group_size, HD)

        def attend(block_args):
            query, key_old, val_old, key_new, val_new, lens = block_args
            query = query.astype(jnp.float32)
            old_scores = jnp.einsum('rkgd,rckd->rkgc', query, key_old.astype(jnp.float32)) * score_scale
            valid_mask = positions[None, :] < lens[:, None]
            old_scores = jnp.where(valid_mask[:, None, None, :], old_scores, NEGATIVE)
            new_scores = jnp.einsum('rkgd,trkd->rkgt', query, key_new.astype(jnp.float32)) * score_scale
            new_scores = jnp.where(section_iota <= section, new_scores, NEGATIVE)
            old_probs, new_probs = softmax_pair(old_scores, new_scores)
            attended = jnp.einsum('rkgc,rckd->rkgd', old_probs.astype(jnp.float32), val_old.astype(jnp.float32))
            attended = attended + jnp.einsum('rkgt,trkd->rkgd', new_probs.astype(jnp.float32), val_new.astype(jnp.float32))
            return attended.astype(jnp.bfloat16).reshape(req_block, H * HD)
        attended = lax.map(attend, (query_blocks, keys_old, vals_old, keys_new, vals_new, lens_block))
        attended = attended.reshape(REQUESTS, H * HD)
        resid = hidden_in[section].astype(jnp.float32) + jnp.dot(attended, out_weight, preferred_element_type=jnp.float32)
        normed = (resid * lax.rsqrt(lax.optimization_barrier(jnp.mean(resid * resid, axis=-1, keepdims=True)) + EPSILON) * gain).astype(jnp.bfloat16)
        expert_ids = routes[section].reshape(source_count, assign)
        hits = (expert_ids[:, :, None] == expert_iota).astype(jnp.int32)
        before = (jnp.cumsum(hits, axis=1) - hits).astype(jnp.int32)
        slot_rank = lax.optimization_barrier(jnp.sum(before * hits, axis=-1)).astype(jnp.int32)
        rows = normed.reshape(source_count, TOK_DEV, D)[:, token_index]
        buffers = jnp.zeros((EXPERTS, source_count, SLOT, D), jnp.bfloat16)
        buffers = buffers.at[expert_ids, source_index, slot_rank].set(rows)

        def expert(block_args):
            rows_in, gate_w, up_w, down_w = block_args
            flat = rows_in.reshape(source_count * SLOT, D)
            outputs = []
            for half_index in range(2):
                lower = half_index * HID_HALF
                gate_act = jnp.dot(flat, gate_w[:, lower:lower + HID_HALF], preferred_element_type=jnp.float32)
                up_act = jnp.dot(flat, up_w[:, lower:lower + HID_HALF], preferred_element_type=jnp.float32)
                activated = (jax.nn.silu(gate_act) * up_act).astype(jnp.bfloat16)
                outputs.append(jnp.dot(activated, down_w[lower:lower + HID_HALF], preferred_element_type=jnp.float32).astype(jnp.bfloat16))
            return jnp.stack(outputs)
        parts = lax.map(expert, (buffers, w_gate, w_up, w_down))
        parts = parts.reshape(EXPERTS, 2, source_count, SLOT, D).transpose(0, 2, 3, 1, 4)
        picked = parts[expert_ids, source_index, slot_rank].astype(jnp.float32)
        combined = (picked[:, :, 0] + picked[:, :, 1]).astype(jnp.bfloat16)
        summed = lax.optimization_barrier(combined).astype(jnp.float32)
        weights = route_weights[section].reshape(source_count, assign)
        mixture = lax.optimization_barrier(jnp.sum((summed * weights[..., None]).reshape(source_count, TOK_DEV, TOPK, D), axis=2))
        mixture = mixture.reshape(REQUESTS, D)
        results.append((resid + mixture).astype(jnp.bfloat16))
    return jnp.stack(results)
```

```python
import math

import jax
import jax.numpy as jnp
from jax import lax
from jax.sharding import PartitionSpec as P

H = 32
KVH = 4
HD = 128


EPSILON = 1e-06
NEGATIVE = -1e30


def softmax_pair(old_scores, new_scores):
    row_max = jnp.maximum(jnp.max(old_scores, axis=-1), jnp.max(new_scores, axis=-1))
    old_exp = jnp.exp(old_scores - row_max[..., None])
    new_exp = jnp.exp(new_scores - row_max[..., None])
    row_total = jnp.sum(old_exp, axis=-1) + jnp.sum(new_exp, axis=-1)
    old_probs = (old_exp / row_total[..., None]).astype(jnp.bfloat16)
    new_probs = (new_exp / row_total[..., None]).astype(jnp.bfloat16)
    return (old_probs, new_probs)


def attend(queries, new_kv, cache, lengths):
    steps, reqs = queries.shape[0], queries.shape[1]
    group = H // KVH
    context = cache.shape[2]
    scale = 1.0 / math.sqrt(HD)
    query = queries.reshape(steps, reqs, group, HD).transpose(1, 0, 2, 3)
    query = query.reshape(reqs, steps * group, HD)
    old_scores = (
        jnp.einsum("rqd,rcd->rqc", query, cache[0], preferred_element_type=jnp.float32) * scale
    )
    valid = jnp.arange(context, dtype=jnp.int32)[None, :] < lengths[:, None]
    old_scores = jnp.where(valid[:, None, :], old_scores, NEGATIVE)
    new_scores = (
        jnp.einsum("rqd,trd->rqt", query, new_kv[:, 0], preferred_element_type=jnp.float32) * scale
    )
    step_of_row = jnp.arange(steps * group, dtype=jnp.int32) // group
    causal = jnp.arange(steps, dtype=jnp.int32)[None, :] <= step_of_row[:, None]
    new_scores = jnp.where(causal[None], new_scores, NEGATIVE)
    old_probs, new_probs = softmax_pair(old_scores, new_scores)
    attended = jnp.einsum("rqc,rcd->rqd", old_probs, cache[1], preferred_element_type=jnp.float32)
    attended = attended + jnp.einsum(
        "rqt,trd->rqd", new_probs, new_kv[:, 1], preferred_element_type=jnp.float32
    )
    return attended.astype(jnp.bfloat16)


def on_device(
    hidden_in,
    queries,
    new_kv,
    cache,
    lengths,
    out_weight,
    norm_gain,
    routes,
    route_weights,
    w_gate,
    w_up,
    w_down,
):
    steps, toks, width = hidden_in.shape
    rows = steps * toks
    reqs = queries.shape[1]
    group = H // KVH
    tp = lax.axis_size("tp")
    experts = lax.axis_size("dp") * tp
    slots = 2
    me = lax.axis_index("tp")

    attended = attend(queries, new_kv, cache, lengths)
    attended = attended.reshape(tp, toks, steps, group * HD).transpose(0, 2, 1, 3)
    projected = jnp.dot(
        attended.reshape(tp * rows, group * HD), out_weight, preferred_element_type=jnp.float32
    ).reshape(tp, rows, width)
    sent = projected.astype(jnp.bfloat16)
    total = lax.dynamic_index_in_dim(projected, me, 0, keepdims=False)
    for hop in range(1, tp):
        block = lax.dynamic_index_in_dim(sent, (me + hop) % tp, 0, keepdims=False)
        total = total + lax.ppermute(
            block, "tp", [(i, (i + hop) % tp) for i in range(tp)]
        ).astype(jnp.float32)
    resid = hidden_in.reshape(rows, width).astype(jnp.float32) + total
    normed = (
        resid
        * lax.rsqrt(jnp.mean(resid * resid, axis=-1, keepdims=True) + EPSILON)
        * norm_gain.astype(jnp.float32)
    ).astype(jnp.bfloat16)

    hits = routes[:, :, :, None] == jnp.arange(experts, dtype=jnp.int32)
    member = jnp.any(hits, axis=2)
    earlier = jnp.cumsum(member.astype(jnp.int32), axis=1) - member.astype(jnp.int32)
    weight = jnp.sum(jnp.where(hits, route_weights[..., None], 0.0), axis=2)
    same_step = jnp.eye(steps, dtype=jnp.bool_)
    place = (
        member[:, :, :, None, None]
        & same_step[:, None, None, :, None]
        & (earlier[:, :, :, None, None] == jnp.arange(slots, dtype=jnp.int32))
    )
    mixer = jnp.where(place, weight[:, :, :, None, None], 0.0).reshape(rows, -1)
    place = place.reshape(rows, experts * steps * slots).astype(jnp.bfloat16)

    outgoing = jnp.einsum("tq,td->qd", place, normed, preferred_element_type=jnp.float32)
    outgoing = outgoing.astype(jnp.bfloat16).reshape(experts, steps * slots, width)
    received = lax.all_to_all(outgoing, ("dp", "tp"), 0, 0, tiled=True).reshape(-1, width)
    swap = [(0, 1), (1, 0)]
    sibling = lax.ppermute(received, "side", swap)

    def half_expert(tokens):
        gate = jnp.dot(tokens, w_gate[0], preferred_element_type=jnp.float32)
        up = jnp.dot(tokens, w_up[0], preferred_element_type=jnp.float32)
        act = (jax.nn.silu(gate) * up).astype(jnp.bfloat16)
        return jnp.dot(act, w_down[0], preferred_element_type=jnp.float32).astype(jnp.bfloat16)

    other_part = lax.ppermute(half_expert(sibling), "side", swap)
    own_part = half_expert(received)
    combined = (own_part.astype(jnp.float32) + other_part.astype(jnp.float32)).astype(jnp.bfloat16)
    returned = lax.all_to_all(
        combined.reshape(experts, steps * slots, width), ("dp", "tp"), 0, 0, tiled=True
    ).reshape(-1, width)

    high = mixer.astype(jnp.bfloat16)
    low = (mixer - high.astype(jnp.float32)).astype(jnp.bfloat16)
    mixed = jnp.dot(
        jnp.concatenate([high, low], axis=0), returned, preferred_element_type=jnp.float32
    )
    mixture = mixed[:rows] + mixed[rows:]
    return (resid + mixture).astype(jnp.bfloat16).reshape(steps, toks, width)


def solution(mesh):
    placed = (
        P(None, ("side", "dp", "tp"), None),
        P(None, ("side", "dp"), "tp"),
        P(None, None, ("side", "dp"), "tp"),
        P(None, ("side", "dp"), None, "tp"),
        P(("side", "dp")),
        P("tp", None),
        P(),
        P(None, ("side", "dp", "tp"), None),
        P(None, ("side", "dp", "tp"), None),
        P(("dp", "tp"), None, "side"),
        P(("dp", "tp"), None, "side"),
        P(("dp", "tp"), "side", None),
    )
    return jax.shard_map(
        on_device,
        mesh=mesh,
        in_specs=placed,
        out_specs=P(None, ("side", "dp", "tp"), None),
        check_vma=False,
    )
```

```python
import math

import jax
import jax.numpy as jnp
from jax import lax
from jax.experimental import pallas as pl
from jax.experimental.pallas import tpu as pltpu
from jax.sharding import PartitionSpec as P

H = 32
KVH = 4
HD = 128


EPSILON = 1e-06
NEGATIVE = -1e30


def softmax_pair(old_scores, new_scores):
    row_max = jnp.maximum(jnp.max(old_scores, axis=-1), jnp.max(new_scores, axis=-1))
    old_exp = jnp.exp(old_scores - row_max[..., None])
    new_exp = jnp.exp(new_scores - row_max[..., None])
    row_total = jnp.sum(old_exp, axis=-1) + jnp.sum(new_exp, axis=-1)
    old_probs = (old_exp / row_total[..., None]).astype(jnp.bfloat16)
    new_probs = (new_exp / row_total[..., None]).astype(jnp.bfloat16)
    return (old_probs, new_probs)


def attend(queries, new_kv, cache, lengths):
    steps, reqs = queries.shape[0], queries.shape[1]
    group = H // KVH
    context = cache.shape[2]
    scale = 1.0 / math.sqrt(HD)
    query = queries.reshape(steps, reqs, group, HD).transpose(1, 0, 2, 3)
    query = query.reshape(reqs, steps * group, HD)
    old_scores = (
        jnp.einsum("rqd,rcd->rqc", query, cache[0], preferred_element_type=jnp.float32) * scale
    )
    valid = jnp.arange(context, dtype=jnp.int32)[None, :] < lengths[:, None]
    old_scores = jnp.where(valid[:, None, :], old_scores, NEGATIVE)
    new_scores = (
        jnp.einsum("rqd,trd->rqt", query, new_kv[:, 0], preferred_element_type=jnp.float32) * scale
    )
    step_of_row = jnp.arange(steps * group, dtype=jnp.int32) // group
    causal = jnp.arange(steps, dtype=jnp.int32)[None, :] <= step_of_row[:, None]
    new_scores = jnp.where(causal[None], new_scores, NEGATIVE)
    old_probs, new_probs = softmax_pair(old_scores, new_scores)
    attended = jnp.einsum("rqc,rcd->rqd", old_probs, cache[1], preferred_element_type=jnp.float32)
    attended = attended + jnp.einsum(
        "rqt,trd->rqd", new_probs, new_kv[:, 1], preferred_element_type=jnp.float32
    )
    return attended.astype(jnp.bfloat16)


def ffn_kernel(x_ref, gate_ref, up_ref, down_ref, *rest):
    x = x_ref[...]
    gate = jnp.dot(x, gate_ref[...], preferred_element_type=jnp.float32)
    up = jnp.dot(x, up_ref[...], preferred_element_type=jnp.float32)
    act = (gate / (1.0 + jnp.exp(-gate)) * up).astype(jnp.bfloat16)
    part = jnp.dot(act, down_ref[...], preferred_element_type=jnp.float32).astype(jnp.bfloat16)
    if len(rest) == 2:
        part = (part.astype(jnp.float32) + rest[0][...].astype(jnp.float32)).astype(jnp.bfloat16)
    rest[-1][...] = part


BLOCK = 256


def half_expert(tokens, first, count, w_gate, w_up, w_down, other=None, out_rows=None):
    width = tokens.shape[1]
    start = first // BLOCK
    shift = 0 if out_rows is None else start
    row = pl.BlockSpec((BLOCK, width), lambda i: (i + start, 0))
    plain = pl.BlockSpec((BLOCK, width), lambda i: (i, 0))
    whole = pl.BlockSpec(memory_space=pltpu.VMEM)
    args = [tokens, w_gate, w_up, w_down]
    specs = [row, whole, whole, whole]
    if other is not None:
        args.append(other)
        specs.append(plain)
    macs = count * width * w_gate.shape[1] * 3
    return pl.pallas_call(
        ffn_kernel,
        grid=(count // BLOCK,),
        in_specs=specs,
        out_specs=pl.BlockSpec((BLOCK, width), lambda i: (i + shift, 0)),
        out_shape=jax.ShapeDtypeStruct((out_rows or count, width), jnp.bfloat16),
        compiler_params=pltpu.CompilerParams(vmem_limit_bytes=16 * 1024 * 1024),
        cost_estimate=pl.CostEstimate(
            flops=2 * macs, bytes_accessed=4 * count * width, transcendentals=count * 640
        ),
        name="half_expert",
    )(*args)


def on_device(
    hidden_in,
    queries,
    new_kv,
    cache,
    lengths,
    out_weight,
    norm_gain,
    routes,
    route_weights,
    w_gate,
    w_up,
    w_down,
):
    steps, toks, width = hidden_in.shape
    rows = steps * toks
    reqs = queries.shape[1]
    group = H // KVH
    tp = lax.axis_size("tp")
    experts = lax.axis_size("dp") * tp
    slots = 2
    me = lax.axis_index("tp")

    attended = attend(queries, new_kv, cache, lengths)
    attended = attended.reshape(tp, toks, steps, group * HD).transpose(0, 2, 1, 3)
    projected = jnp.dot(
        attended.reshape(tp * rows, group * HD), out_weight, preferred_element_type=jnp.float32
    ).reshape(tp, rows, width)
    sent = projected.astype(jnp.bfloat16)
    total = lax.dynamic_index_in_dim(projected, me, 0, keepdims=False)
    for hop in range(1, tp):
        block = lax.dynamic_index_in_dim(sent, (me + hop) % tp, 0, keepdims=False)
        total = total + lax.ppermute(
            block, "tp", [(i, (i + hop) % tp) for i in range(tp)]
        ).astype(jnp.float32)
    resid = hidden_in.reshape(rows, width).astype(jnp.float32) + total
    normed = (
        resid
        * lax.rsqrt(jnp.mean(resid * resid, axis=-1, keepdims=True) + EPSILON)
        * norm_gain.astype(jnp.float32)
    ).astype(jnp.bfloat16)

    hits = routes[:, :, :, None] == jnp.arange(experts, dtype=jnp.int32)
    member = jnp.any(hits, axis=2)
    earlier = jnp.cumsum(member.astype(jnp.int32), axis=1) - member.astype(jnp.int32)
    weight = jnp.sum(jnp.where(hits, route_weights[..., None], 0.0), axis=2)
    same_step = jnp.eye(steps, dtype=jnp.bool_)
    place = (
        member[:, :, :, None, None]
        & same_step[:, None, None, :, None]
        & (earlier[:, :, :, None, None] == jnp.arange(slots, dtype=jnp.int32))
    )
    mixer = jnp.where(place, weight[:, :, :, None, None], 0.0).reshape(rows, -1)
    place = place.reshape(rows, experts * steps * slots).astype(jnp.bfloat16)

    outgoing = jnp.einsum("tq,td->qd", place, normed, preferred_element_type=jnp.float32)
    outgoing = outgoing.astype(jnp.bfloat16).reshape(experts, steps * slots, width)
    received = lax.all_to_all(outgoing, ("dp", "tp"), 0, 0, tiled=True).reshape(-1, width)
    swap = [(0, 1), (1, 0)]
    total_rows = received.shape[0]
    half = total_rows // 2
    weights = (w_gate[0], w_up[0], w_down[0])
    sibling_back = lax.ppermute(received[half:], "side", swap)
    sibling_front = lax.ppermute(received[:half], "side", swap)
    own_front = half_expert(received, 0, half, *weights)
    own_front, sibling_back = lax.optimization_barrier((own_front, sibling_back))
    other_back = lax.ppermute(half_expert(sibling_back, 0, half, *weights), "side", swap)
    other_front = lax.ppermute(half_expert(sibling_front, 0, half, *weights), "side", swap)
    combined = half_expert(received, half, half, *weights, other=other_back, out_rows=total_rows)
    front = own_front.astype(jnp.float32) + other_front.astype(jnp.float32)
    combined = lax.dynamic_update_slice(combined, front.astype(jnp.bfloat16), (0, 0))
    returned = lax.all_to_all(
        combined.reshape(experts, steps * slots, width), ("dp", "tp"), 0, 0, tiled=True
    ).reshape(-1, width)

    high = mixer.astype(jnp.bfloat16)
    low = (mixer - high.astype(jnp.float32)).astype(jnp.bfloat16)
    mixed = jnp.dot(
        jnp.concatenate([high, low], axis=0), returned, preferred_element_type=jnp.float32
    )
    mixture = mixed[:rows] + mixed[rows:]
    return (resid + mixture).astype(jnp.bfloat16).reshape(steps, toks, width)


def solution(mesh):
    placed = (
        P(None, ("side", "dp", "tp"), None),
        P(None, ("side", "dp"), "tp"),
        P(None, None, ("side", "dp"), "tp"),
        P(None, ("side", "dp"), None, "tp"),
        P(("side", "dp")),
        P("tp", None),
        P(),
        P(None, ("side", "dp", "tp"), None),
        P(None, ("side", "dp", "tp"), None),
        P(("dp", "tp"), None, "side"),
        P(("dp", "tp"), None, "side"),
        P(("dp", "tp"), "side", None),
    )
    return jax.shard_map(
        on_device,
        mesh=mesh,
        in_specs=placed,
        out_specs=P(None, ("side", "dp", "tp"), None),
        check_vma=False,
    )
```

```python
import functools
import math

import jax
import jax.numpy as jnp
from jax import lax
from jax.experimental import pallas as pl
from jax.experimental.pallas import tpu as pltpu
from jax.sharding import PartitionSpec as P

HD = 128


EPSILON = 1e-06
NEGATIVE = -1e30


def attend_project_kernel(
    me_ref, lens_ref, query_ref, new_ref, cache_hbm, weight_hbm, *rest
):
    outs, (cache_buf, weight_buf, att_buf, cache_sem, weight_sem) = rest[:-5], rest[-5:]
    parts = len(outs)
    steps, reqs = query_ref.shape[0], query_ref.shape[1]
    toks = reqs // parts
    group = query_ref.shape[2] // HD
    context = cache_buf.shape[3]
    width = weight_hbm.shape[1]
    chunk = width // parts
    rows = steps * toks
    scale = 1.0 / math.sqrt(HD)
    cache_copies = [
        pltpu.make_async_copy(
            cache_hbm.at[:, pl.ds(j * toks, toks)], cache_buf.at[j], cache_sem.at[j]
        )
        for j in range(parts)
    ]
    weight_copies = [
        pltpu.make_async_copy(
            weight_hbm.at[:, pl.ds(n * chunk, chunk)], weight_buf.at[n], weight_sem.at[n]
        )
        for n in range(parts)
    ]
    for copy in cache_copies + weight_copies:
        copy.start()
    me = me_ref[0]
    query = [
        [query_ref[s, :, g * HD : (g + 1) * HD].astype(jnp.float32) for g in range(group)]
        for s in range(steps)
    ]
    new_k = [new_ref[u, 0].astype(jnp.float32) for u in range(steps)]
    new_v = [new_ref[u, 1].astype(jnp.float32) for u in range(steps)]
    tok_old = lax.broadcasted_iota(jnp.int32, (steps * group, toks, context), 1)
    ctx_old = lax.broadcasted_iota(jnp.int32, (steps * group, toks, context), 2)
    shape_new = (steps * group, toks, steps * toks)
    tok_new = lax.broadcasted_iota(jnp.int32, shape_new, 1)
    col_new = lax.broadcasted_iota(jnp.int32, shape_new, 2)
    step_new = lax.broadcasted_iota(jnp.int32, shape_new, 0) // group
    seen = (col_new % toks == tok_new) & (col_new // toks <= step_new)
    for j in range(parts):
        part = slice(j * toks, (j + 1) * toks)
        q = jnp.concatenate([query[s][g][part] for s in range(steps) for g in range(group)], axis=0)
        q = q.astype(jnp.bfloat16)
        k_new = jnp.concatenate([x[part] for x in new_k], axis=0).astype(jnp.bfloat16)
        v_new = jnp.concatenate([x[part] for x in new_v], axis=0).astype(jnp.bfloat16)
        cache_copies[j].wait()
        keys = cache_buf[j, 0].reshape(toks * context, HD)
        contract = (((1,), (1,)), ((), ()))
        every = lax.dot_general(q, keys, contract, preferred_element_type=jnp.float32)
        every = every.reshape(steps * group, toks, toks * context)
        new = lax.dot_general(q, k_new, contract, preferred_element_type=jnp.float32)
        new = jnp.where(seen, new.reshape(shape_new) * scale, NEGATIVE)
        old = every[:, :, 0:context]
        length = jnp.full(tok_old.shape, lens_ref[j * toks], jnp.int32)
        for r in range(1, toks):
            old = jnp.where(tok_old == r, every[:, :, r * context : (r + 1) * context], old)
            length = jnp.where(tok_old == r, lens_ref[j * toks + r], length)
        old = jnp.where(ctx_old < length, old * scale, NEGATIVE)
        row_max = jnp.maximum(
            jnp.max(old, axis=-1, keepdims=True), jnp.max(new, axis=-1, keepdims=True)
        )
        old = jnp.exp(old - row_max)
        new = jnp.exp(new - row_max)
        row_total = jnp.sum(old, axis=-1, keepdims=True) + jnp.sum(new, axis=-1, keepdims=True)
        old = old / row_total
        new = (new / row_total).reshape(rows * group, steps * toks).astype(jnp.bfloat16)
        spread = jnp.concatenate(
            [jnp.where(tok_old == r, old, 0.0) for r in range(toks)], axis=-1
        )
        spread = spread.reshape(rows * group, toks * context).astype(jnp.bfloat16)
        vals = cache_buf[j, 1].reshape(toks * context, HD)
        result = jnp.dot(spread, vals, preferred_element_type=jnp.float32)
        result = result + jnp.dot(new, v_new, preferred_element_type=jnp.float32)
        result = result.reshape(steps, group, toks, HD)
        place = lax.rem(j - me + parts, parts)
        at = pl.ds(pl.multiple_of(place * rows, rows), rows)
        for g in range(group):
            att_buf[at, g * HD : (g + 1) * HD] = (
                result[:, g].reshape(rows, HD).astype(jnp.bfloat16)
            )
    for n in range(parts):
        weight_copies[n].wait()
        block = jnp.dot(att_buf[...], weight_buf[n], preferred_element_type=jnp.float32)
        for k in range(parts):
            outs[k][:, n * chunk : (n + 1) * chunk] = block[k * rows : (k + 1) * rows].astype(
                jnp.bfloat16
            )


def attend_project(queries, new_kv, cache, lengths, out_weight, me, parts):
    steps, reqs, heads_width = queries.shape
    toks = reqs // parts
    context = cache.shape[2]
    width = out_weight.shape[1]
    smem = pl.BlockSpec(memory_space=pltpu.SMEM)
    vmem = pl.BlockSpec(memory_space=pltpu.VMEM)
    hbm = pl.BlockSpec(memory_space=pl.ANY)
    rows = steps * toks
    return pl.pallas_call(
        attend_project_kernel,
        in_specs=[smem, smem, vmem, vmem, hbm, hbm],
        out_specs=[vmem] * parts,
        out_shape=[jax.ShapeDtypeStruct((rows, width), jnp.bfloat16)] * parts,
        scratch_shapes=[
            pltpu.VMEM((parts, 2, toks, context, HD), jnp.bfloat16),
            pltpu.VMEM((parts, heads_width, width // parts), jnp.bfloat16),
            pltpu.VMEM((parts * rows, heads_width), jnp.bfloat16),
            pltpu.SemaphoreType.DMA((parts,)),
            pltpu.SemaphoreType.DMA((parts,)),
        ],
        compiler_params=pltpu.CompilerParams(vmem_limit_bytes=56 * 1024 * 1024),
        name="attend_project",
    )(me.reshape(1), lengths, queries, new_kv, cache, out_weight)


def ffn_kernel(first, count, out_first, x_ref, gate_ref, up_ref, down_ref, *rest):
    out_ref = rest[-1]
    width = down_ref.shape[1]
    x = x_ref[first : first + count, :]
    gate = jnp.dot(x, gate_ref[...], preferred_element_type=jnp.float32)
    up = jnp.dot(x, up_ref[...], preferred_element_type=jnp.float32)
    act = (gate / (1.0 + jnp.exp(-gate)) * up).astype(jnp.bfloat16)
    chunk = width // 4
    for n in range(4):
        cols = slice(n * chunk, (n + 1) * chunk)
        part = jnp.dot(act, down_ref[:, cols], preferred_element_type=jnp.float32)
        part = part.astype(jnp.bfloat16)
        if len(rest) == 2:
            part = part.astype(jnp.float32) + rest[0][:, cols].astype(jnp.float32)
            part = part.astype(jnp.bfloat16)
        out_ref[out_first : out_first + count, cols] = part


def half_expert(tokens, first, count, w_gate, w_up, w_down, other=None, out_rows=None):
    width = tokens.shape[1]
    args = [tokens, w_gate, w_up, w_down] + ([] if other is None else [other])
    macs = count * width * w_gate.shape[1] * 3
    whole = pl.BlockSpec(memory_space=pltpu.VMEM)
    return pl.pallas_call(
        functools.partial(ffn_kernel, first, count, 0 if out_rows is None else first),
        in_specs=[whole] * len(args),
        out_specs=whole,
        out_shape=jax.ShapeDtypeStruct((out_rows or count, width), jnp.bfloat16),
        compiler_params=pltpu.CompilerParams(vmem_limit_bytes=16 * 1024 * 1024),
        cost_estimate=pl.CostEstimate(
            flops=2 * macs, bytes_accessed=4 * count * width, transcendentals=count * 640
        ),
        name="half_expert",
    )(*args)


def on_device(
    hidden_in,
    queries,
    new_kv,
    cache,
    lengths,
    out_weight,
    norm_gain,
    routes,
    route_weights,
    w_gate,
    w_up,
    w_down,
):
    steps, toks, width = hidden_in.shape
    rows = steps * toks
    tp = lax.axis_size("tp")
    experts = lax.axis_size("dp") * tp
    slots = 2
    me = lax.axis_index("tp")

    own, *sent = attend_project(queries, new_kv, cache, lengths, out_weight, me, tp)
    total = own.astype(jnp.float32)
    for hop in range(1, tp):
        total = total + lax.ppermute(
            sent[hop - 1], "tp", [(i, (i + hop) % tp) for i in range(tp)]
        ).astype(jnp.float32)
    resid = hidden_in.reshape(rows, width).astype(jnp.float32) + total
    normed = (
        resid
        * lax.rsqrt(jnp.mean(resid * resid, axis=-1, keepdims=True) + EPSILON)
        * norm_gain.astype(jnp.float32)
    ).astype(jnp.bfloat16)

    hits = routes[:, :, :, None] == jnp.arange(experts, dtype=jnp.int32)
    member = jnp.any(hits, axis=2)
    earlier = jnp.cumsum(member.astype(jnp.int32), axis=1) - member.astype(jnp.int32)
    weight = jnp.sum(jnp.where(hits, route_weights[..., None], 0.0), axis=2)
    same_step = jnp.eye(steps, dtype=jnp.bool_)
    place = (
        member[:, :, :, None, None]
        & same_step[:, None, None, :, None]
        & (earlier[:, :, :, None, None] == jnp.arange(slots, dtype=jnp.int32))
    )
    mixer = jnp.where(place, weight[:, :, :, None, None], 0.0).reshape(rows, -1)
    place = place.reshape(rows, experts * steps * slots).astype(jnp.bfloat16)

    outgoing = jnp.einsum("tq,td->qd", place, normed, preferred_element_type=jnp.float32)
    outgoing = outgoing.astype(jnp.bfloat16)
    high = mixer.astype(jnp.bfloat16)
    mixer = jnp.concatenate([high, (mixer - high.astype(jnp.float32)).astype(jnp.bfloat16)], axis=0)
    outgoing, mixer = lax.optimization_barrier((outgoing, mixer))
    outgoing = outgoing.reshape(experts, steps * slots, width)
    received = lax.all_to_all(outgoing, ("dp", "tp"), 0, 0, tiled=True).reshape(-1, width)
    swap = [(0, 1), (1, 0)]
    total_rows = received.shape[0]
    half = total_rows // 2
    weights = (w_gate[0], w_up[0], w_down[0])
    sibling_back = lax.ppermute(received[half:], "side", swap)
    sibling_front = lax.ppermute(received[:half], "side", swap)
    own_front = half_expert(received, 0, half, *weights)
    own_front, sibling_back = lax.optimization_barrier((own_front, sibling_back))
    other_back = lax.ppermute(half_expert(sibling_back, 0, half, *weights), "side", swap)
    other_front = lax.ppermute(half_expert(sibling_front, 0, half, *weights), "side", swap)
    combined = half_expert(received, half, half, *weights, other=other_back, out_rows=total_rows)
    front = own_front.astype(jnp.float32) + other_front.astype(jnp.float32)
    combined = lax.dynamic_update_slice(combined, front.astype(jnp.bfloat16), (0, 0))
    returned = lax.all_to_all(
        combined.reshape(experts, steps * slots, width), ("dp", "tp"), 0, 0, tiled=True
    ).reshape(-1, width)

    mixed = jnp.dot(mixer, returned, preferred_element_type=jnp.float32)
    mixture = mixed[:rows] + mixed[rows:]
    return (resid + mixture).astype(jnp.bfloat16).reshape(steps, toks, width)


def solution(mesh):
    placed = (
        P(None, ("side", "dp", "tp"), None),
        P(None, ("side", "dp"), "tp"),
        P(None, None, ("side", "dp"), "tp"),
        P(None, ("side", "dp"), None, "tp"),
        P(("side", "dp")),
        P("tp", None),
        P(),
        P(None, ("side", "dp", "tp"), None),
        P(None, ("side", "dp", "tp"), None),
        P(("dp", "tp"), None, "side"),
        P(("dp", "tp"), None, "side"),
        P(("dp", "tp"), "side", None),
    )
    return jax.shard_map(
        on_device,
        mesh=mesh,
        in_specs=placed,
        out_specs=P(None, ("side", "dp", "tp"), None),
        check_vma=False,
    )
```

```python
import functools
import math

import jax
import jax.numpy as jnp
from jax import lax
from jax.experimental import pallas as pl
from jax.experimental.pallas import tpu as pltpu
from jax.sharding import PartitionSpec as P

HD = 128


EPSILON = 1e-06
NEGATIVE = -1e30


def attend_project_kernel(
    me_ref, lens_ref, query_ref, new_ref, cache_hbm, weight_hbm, *rest
):
    outs, rest = rest[:-7], rest[-7:]
    cache_buf, weight_buf, att_buf, stage, cache_sem, weight_sem, out_sem = rest
    parts = len(outs)
    steps, reqs = query_ref.shape[0], query_ref.shape[1]
    toks = reqs // parts
    group = query_ref.shape[2] // HD
    context = cache_buf.shape[3]
    width = weight_hbm.shape[1]
    chunk = width // parts
    rows = steps * toks
    scale = 1.0 / math.sqrt(HD)
    cache_copies = [
        pltpu.make_async_copy(
            cache_hbm.at[:, pl.ds(j * toks, toks)], cache_buf.at[j], cache_sem.at[j]
        )
        for j in range(parts)
    ]
    weight_copies = [
        pltpu.make_async_copy(
            weight_hbm.at[:, pl.ds(n * chunk, chunk)], weight_buf.at[n], weight_sem.at[n]
        )
        for n in range(parts)
    ]
    for copy in cache_copies + weight_copies:
        copy.start()
    me = me_ref[0]
    query = [
        [query_ref[s, :, g * HD : (g + 1) * HD].astype(jnp.float32) for g in range(group)]
        for s in range(steps)
    ]
    new_k = [new_ref[u, 0].astype(jnp.float32) for u in range(steps)]
    new_v = [new_ref[u, 1].astype(jnp.float32) for u in range(steps)]
    lanes = (1, toks, context)
    tok = lax.broadcasted_iota(jnp.int32, lanes, 1)
    col = lax.broadcasted_iota(jnp.int32, lanes, 2)
    is_tok = [tok == r for r in range(toks)]
    same = col % toks == tok
    seen = jnp.concatenate(
        [
            jnp.broadcast_to(jnp.where(same & (col // toks <= s), 0.0, NEGATIVE), (group,) + lanes[1:])
            for s in range(steps)
        ],
        axis=0,
    )
    blank = jnp.zeros((context - steps * toks, HD), jnp.float32)
    for j in range(parts):
        part = slice(j * toks, (j + 1) * toks)
        q = jnp.concatenate([query[s][g][part] for s in range(steps) for g in range(group)], axis=0)
        q = q.astype(jnp.bfloat16)
        k_new = jnp.concatenate([x[part] for x in new_k] + [blank], axis=0).astype(jnp.bfloat16)
        v_new = jnp.concatenate([x[part] for x in new_v] + [blank], axis=0).astype(jnp.bfloat16)
        cache_copies[j].wait()
        keys = cache_buf[j, 0].reshape(toks * context, HD)
        contract = (((1,), (1,)), ((), ()))
        every = lax.dot_general(q, keys, contract, preferred_element_type=jnp.float32)
        every = every.reshape(steps * group, toks, toks * context)
        new = lax.dot_general(q, k_new, contract, preferred_element_type=jnp.float32)
        new = new.reshape(steps * group, toks, context) * scale + seen
        old = every[:, :, 0:context]
        length = jnp.full(lanes, lens_ref[j * toks], jnp.int32)
        for r in range(1, toks):
            old = jnp.where(is_tok[r], every[:, :, r * context : (r + 1) * context], old)
            length = jnp.where(is_tok[r], lens_ref[j * toks + r], length)
        old = jnp.where(col < length, old * scale, NEGATIVE)
        row_max = jnp.max(jnp.maximum(old, new), axis=-1, keepdims=True)
        old = jnp.exp(old - row_max)
        new = jnp.exp(new - row_max)
        inverse = 1.0 / jnp.sum(old + new, axis=-1, keepdims=True)
        old = old * inverse
        new = (new * inverse).reshape(rows * group, context).astype(jnp.bfloat16)
        spread = jnp.concatenate([jnp.where(is_tok[r], old, 0.0) for r in range(toks)], axis=-1)
        spread = spread.reshape(rows * group, toks * context).astype(jnp.bfloat16)
        vals = cache_buf[j, 1].reshape(toks * context, HD)
        result = jnp.dot(spread, vals, preferred_element_type=jnp.float32)
        result = result + jnp.dot(new, v_new, preferred_element_type=jnp.float32)
        result = result.reshape(steps, group, toks, HD)
        place = lax.rem(j - me + parts, parts)
        at = pl.ds(pl.multiple_of(place * rows, rows), rows)
        for g in range(group):
            att_buf[at, g * HD : (g + 1) * HD] = (
                result[:, g].reshape(rows, HD).astype(jnp.bfloat16)
            )
    out_copies = []
    for n in range(parts):
        weight_copies[n].wait()
        block = jnp.dot(att_buf[...], weight_buf[n], preferred_element_type=jnp.float32)
        cols = pl.ds(n * chunk, chunk)
        for k in range(parts):
            stage[k, :, n * chunk : (n + 1) * chunk] = block[k * rows : (k + 1) * rows].astype(
                jnp.bfloat16
            )
            copy = pltpu.make_async_copy(
                stage.at[k, :, cols], outs[k].at[:, cols], out_sem.at[k, n]
            )
            copy.start()
            out_copies.append(copy)
    for copy in out_copies:
        copy.wait()


def attend_project(queries, new_kv, cache, lengths, out_weight, me, parts):
    steps, reqs, heads_width = queries.shape
    toks = reqs // parts
    context = cache.shape[2]
    width = out_weight.shape[1]
    smem = pl.BlockSpec(memory_space=pltpu.SMEM)
    vmem = pl.BlockSpec(memory_space=pltpu.VMEM)
    hbm = pl.BlockSpec(memory_space=pl.ANY)
    rows = steps * toks
    return pl.pallas_call(
        attend_project_kernel,
        in_specs=[smem, smem, vmem, vmem, hbm, hbm],
        out_specs=[hbm] * parts,
        out_shape=[jax.ShapeDtypeStruct((rows, width), jnp.bfloat16)] * parts,
        scratch_shapes=[
            pltpu.VMEM((parts, 2, toks, context, HD), jnp.bfloat16),
            pltpu.VMEM((parts, heads_width, width // parts), jnp.bfloat16),
            pltpu.VMEM((parts * rows, heads_width), jnp.bfloat16),
            pltpu.VMEM((parts, rows, width), jnp.bfloat16),
            pltpu.SemaphoreType.DMA((parts,)),
            pltpu.SemaphoreType.DMA((parts,)),
            pltpu.SemaphoreType.DMA((parts, parts)),
        ],
        compiler_params=pltpu.CompilerParams(vmem_limit_bytes=56 * 1024 * 1024),
        name="attend_project",
    )(me.reshape(1), lengths, queries, new_kv, cache, out_weight)


def ffn_kernel(first, count, out_first, x_ref, gate_ref, up_ref, down_ref, *rest):
    out_ref = rest[-1]
    width = down_ref.shape[1]
    x = x_ref[first : first + count, :]
    gate = jnp.dot(x, gate_ref[...], preferred_element_type=jnp.float32)
    up = jnp.dot(x, up_ref[...], preferred_element_type=jnp.float32)
    act = (gate / (1.0 + jnp.exp(-gate)) * up).astype(jnp.bfloat16)
    chunk = width // 8
    for n in range(8):
        cols = slice(n * chunk, (n + 1) * chunk)
        part = jnp.dot(act, down_ref[:, cols], preferred_element_type=jnp.float32)
        part = part.astype(jnp.bfloat16)
        if len(rest) == 2:
            part = part.astype(jnp.float32) + rest[0][:, cols].astype(jnp.float32)
            part = part.astype(jnp.bfloat16)
        out_ref[out_first : out_first + count, cols] = part


def half_expert(tokens, first, count, w_gate, w_up, w_down, other=None, out_rows=None):
    width = tokens.shape[1]
    args = [tokens, w_gate, w_up, w_down] + ([] if other is None else [other])
    macs = count * width * w_gate.shape[1] * 3
    whole = pl.BlockSpec(memory_space=pltpu.VMEM)
    return pl.pallas_call(
        functools.partial(ffn_kernel, first, count, 0 if out_rows is None else first),
        in_specs=[whole] * len(args),
        out_specs=whole,
        out_shape=jax.ShapeDtypeStruct((out_rows or count, width), jnp.bfloat16),
        compiler_params=pltpu.CompilerParams(vmem_limit_bytes=16 * 1024 * 1024),
        cost_estimate=pl.CostEstimate(
            flops=2 * macs, bytes_accessed=4 * count * width, transcendentals=count * 640
        ),
        name="half_expert",
    )(*args)


def mix_kernel(mixer_ref, returned_ref, resid_ref, out_ref):
    rows = resid_ref.shape[0]
    mixed = jnp.dot(mixer_ref[...], returned_ref[...], preferred_element_type=jnp.float32)
    out_ref[...] = (resid_ref[...] + (mixed[:rows] + mixed[rows:])).astype(jnp.bfloat16)


def mix(mixer, returned, resid):
    rows, width = resid.shape
    return pl.pallas_call(
        mix_kernel,
        in_specs=[
            pl.BlockSpec(memory_space=pltpu.VMEM),
            pl.BlockSpec(memory_space=pltpu.VMEM),
            pl.BlockSpec(memory_space=pltpu.VMEM),
        ],
        out_specs=pl.BlockSpec(memory_space=pltpu.VMEM),
        out_shape=jax.ShapeDtypeStruct((rows, width), jnp.bfloat16),
        compiler_params=pltpu.CompilerParams(vmem_limit_bytes=16 * 1024 * 1024),
        name="mix",
    )(mixer, returned, resid)


def on_device(
    hidden_in,
    queries,
    new_kv,
    cache,
    lengths,
    out_weight,
    norm_gain,
    routes,
    route_weights,
    w_gate,
    w_up,
    w_down,
):
    steps, toks, width = hidden_in.shape
    rows = steps * toks
    tp = lax.axis_size("tp")
    experts = lax.axis_size("dp") * tp
    slots = 2
    me = lax.axis_index("tp")

    own, *sent = attend_project(queries, new_kv, cache, lengths, out_weight, me, tp)
    total = own.astype(jnp.float32)
    for hop in range(1, tp):
        total = total + lax.ppermute(
            sent[hop - 1], "tp", [(i, (i + hop) % tp) for i in range(tp)]
        ).astype(jnp.float32)
    resid = hidden_in.reshape(rows, width).astype(jnp.float32) + total
    normed = (
        resid
        * lax.rsqrt(jnp.mean(resid * resid, axis=-1, keepdims=True) + EPSILON)
        * norm_gain.astype(jnp.float32)
    ).astype(jnp.bfloat16)

    hits = routes[:, :, :, None] == jnp.arange(experts, dtype=jnp.int32)
    member = jnp.any(hits, axis=2)
    earlier = jnp.cumsum(member.astype(jnp.int32), axis=1) - member.astype(jnp.int32)
    weight = jnp.sum(jnp.where(hits, route_weights[..., None], 0.0), axis=2)
    same_step = jnp.eye(steps, dtype=jnp.bool_)
    place = (
        member[:, :, :, None, None]
        & same_step[:, None, None, :, None]
        & (earlier[:, :, :, None, None] == jnp.arange(slots, dtype=jnp.int32))
    )
    mixer = jnp.where(place, weight[:, :, :, None, None], 0.0).reshape(rows, -1)
    place = place.reshape(rows, experts * steps * slots).astype(jnp.bfloat16)

    outgoing = jnp.einsum("tq,td->qd", place, normed, preferred_element_type=jnp.float32)
    outgoing = outgoing.astype(jnp.bfloat16)
    high = mixer.astype(jnp.bfloat16)
    mixer = jnp.concatenate([high, (mixer - high.astype(jnp.float32)).astype(jnp.bfloat16)], axis=0)
    outgoing, mixer = lax.optimization_barrier((outgoing, mixer))
    outgoing = outgoing.reshape(experts, steps * slots, width)
    received = lax.all_to_all(outgoing, ("dp", "tp"), 0, 0, tiled=True).reshape(-1, width)
    swap = [(0, 1), (1, 0)]
    total_rows = received.shape[0]
    half = total_rows // 2
    weights = (w_gate[0], w_up[0], w_down[0])
    sibling_back = lax.ppermute(received[half:], "side", swap)
    sibling_front = lax.ppermute(received[:half], "side", swap)
    own_front = half_expert(received, 0, half, *weights)
    own_front, sibling_back = lax.optimization_barrier((own_front, sibling_back))
    other_back = lax.ppermute(half_expert(sibling_back, 0, half, *weights), "side", swap)
    other_front = lax.ppermute(half_expert(sibling_front, 0, half, *weights), "side", swap)
    combined = half_expert(received, half, half, *weights, other=other_back, out_rows=total_rows)
    front = own_front.astype(jnp.float32) + other_front.astype(jnp.float32)
    combined = lax.dynamic_update_slice(combined, front.astype(jnp.bfloat16), (0, 0))
    returned = lax.all_to_all(
        combined.reshape(experts, steps * slots, width), ("dp", "tp"), 0, 0, tiled=True
    ).reshape(-1, width)

    return mix(mixer, returned, resid).reshape(steps, toks, width)


def solution(mesh):
    placed = (
        P(None, ("side", "dp", "tp"), None),
        P(None, ("side", "dp"), "tp"),
        P(None, None, ("side", "dp"), "tp"),
        P(None, ("side", "dp"), None, "tp"),
        P(("side", "dp")),
        P("tp", None),
        P(),
        P(None, ("side", "dp", "tp"), None),
        P(None, ("side", "dp", "tp"), None),
        P(("dp", "tp"), None, "side"),
        P(("dp", "tp"), None, "side"),
        P(("dp", "tp"), "side", None),
    )
    return jax.shard_map(
        on_device,
        mesh=mesh,
        in_specs=placed,
        out_specs=P(None, ("side", "dp", "tp"), None),
        check_vma=False,
    )
```

```python
import functools
import math

import jax
import jax.numpy as jnp
from jax import lax
from jax.experimental import pallas as pl
from jax.experimental.pallas import tpu as pltpu
from jax.sharding import PartitionSpec as P

HD = 128


EPSILON = 1e-06
NEGATIVE = -1e30


def attend_project_kernel(
    me_ref, lens_ref, query_ref, new_ref, cache_hbm, weight_hbm, *rest
):
    outs, rest = rest[:-7], rest[-7:]
    cache_buf, weight_buf, att_buf, stage, cache_sem, weight_sem, out_sem = rest
    parts = len(outs)
    steps, reqs = query_ref.shape[0], query_ref.shape[1]
    toks = reqs // parts
    group = query_ref.shape[2] // HD
    context = cache_buf.shape[3]
    width = weight_hbm.shape[1]
    chunk = width // parts
    rows = steps * toks
    scale = 1.0 / math.sqrt(HD)
    cache_copies = [
        pltpu.make_async_copy(
            cache_hbm.at[:, pl.ds(j * toks, toks)], cache_buf.at[j], cache_sem.at[j]
        )
        for j in range(parts)
    ]
    weight_copies = [
        pltpu.make_async_copy(
            weight_hbm.at[:, pl.ds(n * chunk, chunk)], weight_buf.at[n], weight_sem.at[n]
        )
        for n in range(parts)
    ]
    for copy in cache_copies + weight_copies:
        copy.start()
    me = me_ref[0]
    query = [
        [query_ref[s, :, g * HD : (g + 1) * HD].astype(jnp.float32) for g in range(group)]
        for s in range(steps)
    ]
    new_k = [new_ref[u, 0].astype(jnp.float32) for u in range(steps)]
    new_v = [new_ref[u, 1].astype(jnp.float32) for u in range(steps)]
    lanes = (1, toks, context)
    tok = lax.broadcasted_iota(jnp.int32, lanes, 1)
    col = lax.broadcasted_iota(jnp.int32, lanes, 2)
    is_tok = [tok == r for r in range(toks)]
    same = col % toks == tok
    seen = jnp.concatenate(
        [
            jnp.broadcast_to(jnp.where(same & (col // toks <= s), 0.0, NEGATIVE), (group,) + lanes[1:])
            for s in range(steps)
        ],
        axis=0,
    )
    blank = jnp.zeros((context - steps * toks, HD), jnp.float32)
    for j in range(parts):
        part = slice(j * toks, (j + 1) * toks)
        q = jnp.concatenate([query[s][g][part] for s in range(steps) for g in range(group)], axis=0)
        q = q.astype(jnp.bfloat16)
        k_new = jnp.concatenate([x[part] for x in new_k] + [blank], axis=0).astype(jnp.bfloat16)
        v_new = jnp.concatenate([x[part] for x in new_v] + [blank], axis=0).astype(jnp.bfloat16)
        cache_copies[j].wait()
        keys = cache_buf[j, 0].reshape(toks * context, HD)
        contract = (((1,), (1,)), ((), ()))
        every = lax.dot_general(q, keys, contract, preferred_element_type=jnp.float32)
        every = every.reshape(steps * group, toks, toks * context)
        new = lax.dot_general(q, k_new, contract, preferred_element_type=jnp.float32)
        new = new.reshape(steps * group, toks, context) * scale + seen
        old = every[:, :, 0:context]
        length = jnp.full(lanes, lens_ref[j * toks], jnp.int32)
        for r in range(1, toks):
            old = jnp.where(is_tok[r], every[:, :, r * context : (r + 1) * context], old)
            length = jnp.where(is_tok[r], lens_ref[j * toks + r], length)
        old = jnp.where(col < length, old * scale, NEGATIVE)
        row_max = jnp.max(jnp.maximum(old, new), axis=-1, keepdims=True)
        old = jnp.exp(old - row_max)
        new = jnp.exp(new - row_max)
        inverse = 1.0 / jnp.sum(old + new, axis=-1, keepdims=True)
        old = old * inverse
        new = (new * inverse).reshape(rows * group, context).astype(jnp.bfloat16)
        spread = jnp.concatenate([jnp.where(is_tok[r], old, 0.0) for r in range(toks)], axis=-1)
        spread = spread.reshape(rows * group, toks * context).astype(jnp.bfloat16)
        vals = cache_buf[j, 1].reshape(toks * context, HD)
        result = jnp.dot(spread, vals, preferred_element_type=jnp.float32)
        result = result + jnp.dot(new, v_new, preferred_element_type=jnp.float32)
        result = result.reshape(steps, group, toks, HD)
        place = lax.rem(j - me + parts, parts)
        at = pl.ds(pl.multiple_of(place * rows, rows), rows)
        for g in range(group):
            att_buf[at, g * HD : (g + 1) * HD] = (
                result[:, g].reshape(rows, HD).astype(jnp.bfloat16)
            )
    out_copies = []
    for n in range(parts):
        weight_copies[n].wait()
        block = jnp.dot(att_buf[...], weight_buf[n], preferred_element_type=jnp.float32)
        cols = pl.ds(n * chunk, chunk)
        for k in range(parts):
            stage[k, :, n * chunk : (n + 1) * chunk] = block[k * rows : (k + 1) * rows].astype(
                jnp.bfloat16
            )
            copy = pltpu.make_async_copy(
                stage.at[k, :, cols], outs[k].at[:, cols], out_sem.at[k, n]
            )
            copy.start()
            out_copies.append(copy)
    for copy in out_copies:
        copy.wait()


def attend_project(queries, new_kv, cache, lengths, out_weight, me, parts):
    steps, reqs, heads_width = queries.shape
    toks = reqs // parts
    context = cache.shape[2]
    width = out_weight.shape[1]
    smem = pl.BlockSpec(memory_space=pltpu.SMEM)
    vmem = pl.BlockSpec(memory_space=pltpu.VMEM)
    hbm = pl.BlockSpec(memory_space=pl.ANY)
    rows = steps * toks
    return pl.pallas_call(
        attend_project_kernel,
        in_specs=[smem, smem, vmem, vmem, hbm, hbm],
        out_specs=[hbm] * parts,
        out_shape=[jax.ShapeDtypeStruct((rows, width), jnp.bfloat16)] * parts,
        scratch_shapes=[
            pltpu.VMEM((parts, 2, toks, context, HD), jnp.bfloat16),
            pltpu.VMEM((parts, heads_width, width // parts), jnp.bfloat16),
            pltpu.VMEM((parts * rows, heads_width), jnp.bfloat16),
            pltpu.VMEM((parts, rows, width), jnp.bfloat16),
            pltpu.SemaphoreType.DMA((parts,)),
            pltpu.SemaphoreType.DMA((parts,)),
            pltpu.SemaphoreType.DMA((parts, parts)),
        ],
        compiler_params=pltpu.CompilerParams(vmem_limit_bytes=56 * 1024 * 1024),
        name="attend_project",
    )(me.reshape(1), lengths, queries, new_kv, cache, out_weight)


def ffn_kernel(first, count, out_first, x_ref, gate_ref, up_ref, down_ref, *rest):
    out_ref = rest[-1]
    width = down_ref.shape[1]
    x = x_ref[first : first + count, :]
    gate = jnp.dot(x, gate_ref[...], preferred_element_type=jnp.float32)
    up = jnp.dot(x, up_ref[...], preferred_element_type=jnp.float32)
    act = (gate / (1.0 + jnp.exp(-gate)) * up).astype(jnp.bfloat16)
    chunk = width // 8
    for n in range(8):
        cols = slice(n * chunk, (n + 1) * chunk)
        part = jnp.dot(act, down_ref[:, cols], preferred_element_type=jnp.float32)
        part = part.astype(jnp.bfloat16)
        if len(rest) == 2:
            part = part.astype(jnp.float32) + rest[0][:, cols].astype(jnp.float32)
            part = part.astype(jnp.bfloat16)
        out_ref[out_first : out_first + count, cols] = part


def half_expert(tokens, first, count, w_gate, w_up, w_down, other=None, out_rows=None):
    width = tokens.shape[1]
    args = [tokens, w_gate, w_up, w_down] + ([] if other is None else [other])
    macs = count * width * w_gate.shape[1] * 3
    whole = pl.BlockSpec(memory_space=pltpu.VMEM)
    return pl.pallas_call(
        functools.partial(ffn_kernel, first, count, 0 if out_rows is None else first),
        in_specs=[whole] * len(args),
        out_specs=whole,
        out_shape=jax.ShapeDtypeStruct((out_rows or count, width), jnp.bfloat16),
        compiler_params=pltpu.CompilerParams(vmem_limit_bytes=16 * 1024 * 1024),
        cost_estimate=pl.CostEstimate(
            flops=2 * macs, bytes_accessed=4 * count * width, transcendentals=count * 640
        ),
        name="half_expert",
    )(*args)


def mix_kernel(mixer_ref, returned_ref, resid_ref, out_ref):
    rows = resid_ref.shape[0]
    mixed = jnp.dot(mixer_ref[...], returned_ref[...], preferred_element_type=jnp.float32)
    out_ref[...] = (resid_ref[...] + (mixed[:rows] + mixed[rows:])).astype(jnp.bfloat16)


def mix(mixer, returned, resid):
    rows, width = resid.shape
    return pl.pallas_call(
        mix_kernel,
        in_specs=[
            pl.BlockSpec(memory_space=pltpu.VMEM),
            pl.BlockSpec(memory_space=pltpu.VMEM),
            pl.BlockSpec(memory_space=pltpu.VMEM),
        ],
        out_specs=pl.BlockSpec(memory_space=pltpu.VMEM),
        out_shape=jax.ShapeDtypeStruct((rows, width), jnp.bfloat16),
        compiler_params=pltpu.CompilerParams(vmem_limit_bytes=16 * 1024 * 1024),
        name="mix",
    )(mixer, returned, resid)


def on_device(
    hidden_in,
    queries,
    new_kv,
    cache,
    lengths,
    out_weight,
    norm_gain,
    routes,
    route_weights,
    w_gate,
    w_up,
    w_down,
):
    steps, toks, width = hidden_in.shape
    rows = steps * toks
    tp = lax.axis_size("tp")
    experts = lax.axis_size("dp") * tp
    slots = 2
    me = lax.axis_index("tp")

    own, *sent = attend_project(queries, new_kv, cache, lengths, out_weight, me, tp)
    total = own.astype(jnp.float32)
    for hop in sorted(range(1, tp), key=lambda k: min(k, tp - k)):
        total = total + lax.ppermute(
            sent[hop - 1], "tp", [(i, (i + hop) % tp) for i in range(tp)]
        ).astype(jnp.float32)
    resid = hidden_in.reshape(rows, width).astype(jnp.float32) + total
    normed = (
        resid
        * lax.rsqrt(jnp.mean(resid * resid, axis=-1, keepdims=True) + EPSILON)
        * norm_gain.astype(jnp.float32)
    ).astype(jnp.bfloat16)

    hits = routes[:, :, :, None] == jnp.arange(experts, dtype=jnp.int32)
    member = jnp.any(hits, axis=2)
    earlier = jnp.cumsum(member.astype(jnp.int32), axis=1) - member.astype(jnp.int32)
    weight = jnp.sum(jnp.where(hits, route_weights[..., None], 0.0), axis=2)
    same_step = jnp.eye(steps, dtype=jnp.bool_)
    place = (
        member[:, :, :, None, None]
        & same_step[:, None, None, :, None]
        & (earlier[:, :, :, None, None] == jnp.arange(slots, dtype=jnp.int32))
    )
    mixer = jnp.where(place, weight[:, :, :, None, None], 0.0).reshape(rows, -1)
    place = place.reshape(rows, experts * steps * slots).astype(jnp.bfloat16)

    outgoing = jnp.einsum("tq,td->qd", place, normed, preferred_element_type=jnp.float32)
    outgoing = outgoing.astype(jnp.bfloat16)
    high = mixer.astype(jnp.bfloat16)
    mixer = jnp.concatenate([high, (mixer - high.astype(jnp.float32)).astype(jnp.bfloat16)], axis=0)
    outgoing, mixer = lax.optimization_barrier((outgoing, mixer))
    outgoing = outgoing.reshape(experts, steps * slots, width)
    received = lax.all_to_all(outgoing, ("dp", "tp"), 0, 0, tiled=True).reshape(-1, width)
    swap = [(0, 1), (1, 0)]
    total_rows = received.shape[0]
    half = total_rows // 2
    weights = (w_gate[0], w_up[0], w_down[0])
    sibling_back = lax.ppermute(received[half:], "side", swap)
    sibling_front = lax.ppermute(received[:half], "side", swap)
    own_front = half_expert(received, 0, half, *weights)
    own_front, sibling_back = lax.optimization_barrier((own_front, sibling_back))
    other_back = lax.ppermute(half_expert(sibling_back, 0, half, *weights), "side", swap)
    other_front = lax.ppermute(half_expert(sibling_front, 0, half, *weights), "side", swap)
    combined = half_expert(received, half, half, *weights, other=other_back, out_rows=total_rows)
    front = own_front.astype(jnp.float32) + other_front.astype(jnp.float32)
    combined = lax.dynamic_update_slice(combined, front.astype(jnp.bfloat16), (0, 0))
    returned = lax.all_to_all(
        combined.reshape(experts, steps * slots, width), ("dp", "tp"), 0, 0, tiled=True
    ).reshape(-1, width)

    return mix(mixer, returned, resid).reshape(steps, toks, width)


def solution(mesh):
    placed = (
        P(None, ("side", "dp", "tp"), None),
        P(None, ("side", "dp"), "tp"),
        P(None, None, ("side", "dp"), "tp"),
        P(None, ("side", "dp"), None, "tp"),
        P(("side", "dp")),
        P("tp", None),
        P(),
        P(None, ("side", "dp", "tp"), None),
        P(None, ("side", "dp", "tp"), None),
        P(("dp", "tp"), None, "side"),
        P(("dp", "tp"), None, "side"),
        P(("dp", "tp"), "side", None),
    )
    return jax.shard_map(
        on_device,
        mesh=mesh,
        in_specs=placed,
        out_specs=P(None, ("side", "dp", "tp"), None),
        check_vma=False,
    )
```
